512 devices in a mesh: dx: 16 (over z), dy: 4 (over y), band: 8 (over x, core).
Axes of the slice: x: 4, y: 4, z: 16, core: 2. Of those that a mesh axis runs over, the one named last changes fastest.
Arguments:
- vectors: bfloat16 [13, 512, 8192], P(None, 'band', ('dx', 'dy')), may hold values from -6 to 6
- inner_pairs: int32 [6, 8192], P(None, ('dx', 'dy')), may hold values from 0 to 127
- inner_count: int32 [8192], P(('dx', 'dy')), may hold values from 1 to 6, as said below
- inner_blocks: bfloat16 [6, 13, 13, 8192], P(None, None, None, ('dx', 'dy'))
- cross_x_blocks: bfloat16 [4, 13, 13, 1024], P(None, None, None, ('dx', 'dy'))
- cross_y_blocks: bfloat16 [4, 13, 13, 1024], P(None, None, None, ('dx', 'dy'))
- spectrum_top: float32 [1], replicated, may hold values from 8 to 12
- filter_cut: float32 [1], replicated, may hold values from -2 to -0.5
Outputs:
- filtered: bfloat16 [13, 512, 8192], P(None, 'band', ('dx', 'dy'))
- correlation: float32 [512, 512], P('band', ('dx', 'dy'))
- projected: float32 [512, 512], P('band', ('dx', 'dy'))
The draws below stay inside these ranges and needn't reach their ends.
Inputs may be any that keep to these rules, and one draw needn't show every extreme that they name: `inner_count`: slots from an atom's count on are padding; some atom has all 6 slots live.
All inputs are finite; a program needn't handle non-finite values.
Results may differ from the reference program's by a relative error of at most 0.0083.
Values may be sent and summed in bfloat16 or wider, within the bound.
A program may use at most 64 MiB of HBM per device.

```python
import math
import jax
import jax.numpy as jnp

ORB = 13
NVEC = 512
ATOMS_DEV = 128
INNER = 6
BAND_W = 4
GROUP = 8
ATOMS = 8192
EDGE = 1024
N_DX = 16
N_DY = 4


def coupling(key, shape):
    first_key, second_key = jax.random.split(key)
    entries = jax.random.normal(first_key, shape, jnp.float32)
    scales = jnp.exp(jax.random.uniform(second_key, (shape[-1],), jnp.float32, math.log(0.5), math.log(2.0)))
    return (entries * scales / math.sqrt(ORB * 16.0)).astype(jnp.bfloat16)


def draw_inner_count(key, part):
    keys = jax.random.split(jax.random.fold_in(key, 11), 4)
    domains = ATOMS // ATOMS_DEV
    density = jax.random.randint(keys[0], (domains,), 2, INNER + 1)
    density = density.at[jax.random.randint(keys[1], (), 0, domains)].set(INNER)
    per_atom = jnp.repeat(density, ATOMS_DEV, total_repeat_length=ATOMS)
    raw_draw = jax.random.randint(keys[2], (ATOMS,), 0, 1 << 20)
    counts = 1 + raw_draw % per_atom
    counts = counts.at[jax.random.randint(keys[3], (), 0, ATOMS)].set(INNER)
    return counts.astype(jnp.int32)


def draw_inner_blocks(key, part):
    return coupling(jax.random.fold_in(key, 21), (INNER, ORB, ORB, ATOMS))


def draw_cross_x_blocks(key, part):
    return coupling(jax.random.fold_in(key, 31), (BAND_W, ORB, ORB, EDGE))


def draw_cross_y_blocks(key, part):
    return coupling(jax.random.fold_in(key, 41), (BAND_W, ORB, ORB, EDGE))


def plant(values, own_key, smallest, largest):
    dims = values.shape
    place = [jax.random.randint(jax.random.fold_in(own_key, axis), (), 0, dims[axis]) for axis in range(len(dims))]
    values = values.at[tuple(place)].set(smallest)
    longest = dims.index(max(dims))
    place[longest] = (place[longest] + 1) % dims[longest]
    return values.at[tuple(place)].set(largest)


def level_of(key, dims, pieces, least, high):
    gain = 1.0
    for position, parts in pieces:
        draws = jax.random.uniform(jax.random.fold_in(jax.random.fold_in(key, 6), position), (parts,), jnp.float32, least / len(pieces), high / len(pieces))
        gain = gain * jnp.repeat(jnp.exp(draws), dims[position] // parts).reshape((-1,) + (1,) * (len(dims) - 1 - position))
    return gain


def noise(own_key, shape, deviation, bound, cuts=(), held_as=jnp.bfloat16):
    drawn = deviation * jax.random.normal(own_key, shape, jnp.float32)
    if cuts:
        drawn = drawn * level_of(own_key, shape, cuts, -0.22, 0.18)
    return jnp.clip(drawn, -bound, bound).astype(held_as)


def setup_inputs(seed: int = 0) -> dict:
    arg_keys = jax.random.split(jax.random.key(seed), 9)
    return {
        "vectors": noise(arg_keys[0], (ORB, NVEC, ATOMS), 1.0, 6.0, ((1, 8), (2, 64))),
        "inner_pairs": plant(jax.random.randint(arg_keys[1], (INNER, ATOMS), 0, ATOMS_DEV), jax.random.fold_in(arg_keys[1], 1), 0, ATOMS_DEV - 1).astype(jnp.int32),
        "inner_count": draw_inner_count(jax.random.fold_in(arg_keys[8], 71), 0),
        "inner_blocks": draw_inner_blocks(jax.random.fold_in(arg_keys[8], 71), 0),
        "cross_x_blocks": draw_cross_x_blocks(jax.random.fold_in(arg_keys[8], 71), 0),
        "cross_y_blocks": draw_cross_y_blocks(jax.random.fold_in(arg_keys[8], 71), 0),
        "spectrum_top": jnp.clip(jax.random.uniform(arg_keys[6], (1,), jnp.float32, 8.0, 12.0), 8.0, 12.0),
        "filter_cut": jnp.clip(jax.random.uniform(arg_keys[7], (1,), jnp.float32, -2.0, -0.5), -2.0, -0.5),
    }


def apply_ham(field_in, inner_f, partner, cross_sets):
    values = field_in.astype(jnp.float32)
    summed = jnp.zeros(values.shape, jnp.float32)
    for slot_k in range(INNER):
        block_k = inner_f[slot_k]
        summed = summed + jnp.einsum('opa,pva->ova', block_k, values[:, :, partner[slot_k]])
        summed = summed.at[:, :, partner[slot_k]].add(jnp.einsum('opa,ova->pva', block_k, values))
    for blocks_f, row_index, col_lists in cross_sets:
        for offset in range(BAND_W):
            block_m = blocks_f[offset]
            col_index = col_lists[offset]
            summed = summed.at[:, :, row_index].add(jnp.einsum('opt,pvt->ovt', block_m, values[:, :, col_index]))
            summed = summed.at[:, :, col_index].add(jnp.einsum('opt,ovt->pvt', block_m, values[:, :, row_index]))
    return summed


def reference(vectors, inner_pairs, inner_count, inner_blocks, cross_x_blocks, cross_y_blocks, spectrum_top, filter_cut):
    domain_count = N_DX * N_DY
    domain_base = (jnp.arange(ATOMS, dtype=jnp.int32) // ATOMS_DEV) * ATOMS_DEV
    partner = (domain_base[None, :] + inner_pairs).astype(jnp.int32)
    live_mask = (jnp.arange(INNER, dtype=jnp.int32)[:, None] < inner_count[None, :]).astype(jnp.float32)
    inner_f = inner_blocks.astype(jnp.float32) * live_mask[:, None, None, :]
    domains = jnp.arange(domain_count, dtype=jnp.int32)
    first_axis = domains // N_DY
    second_axis = domains % N_DY
    east_domain = ((first_axis + 1) % N_DX) * N_DY + second_axis
    north_domain = first_axis * N_DY + (second_axis + 1) % N_DY
    places = jnp.arange(2 * GROUP, dtype=jnp.int32)
    rim_start = ATOMS_DEV - 8 * GROUP
    lo_x = rim_start + places
    hi_x = rim_start + 2 * GROUP + places
    lo_y = rim_start + 4 * GROUP + places
    hi_y = rim_start + 6 * GROUP + places
    rows_x = (domains[:, None] * ATOMS_DEV + hi_x[None, :]).reshape(-1).astype(jnp.int32)
    rows_y = (domains[:, None] * ATOMS_DEV + hi_y[None, :]).reshape(-1).astype(jnp.int32)
    cols_x = []
    cols_y = []
    for offset in range(BAND_W):
        moved = (places + offset) % (2 * GROUP)
        cols_x.append((east_domain[:, None] * ATOMS_DEV + lo_x[moved][None, :]).reshape(-1).astype(jnp.int32))
        cols_y.append((north_domain[:, None] * ATOMS_DEV + lo_y[moved][None, :]).reshape(-1).astype(jnp.int32))
    cross_sets = ((cross_x_blocks.astype(jnp.float32), rows_x, cols_x), (cross_y_blocks.astype(jnp.float32), rows_y, cols_y))
    top_value = spectrum_top[0]
    cut_value = filter_cut[0]
    half_span = (top_value - cut_value) * 0.5
    centre = (top_value + cut_value) * 0.5
    start_f = vectors.astype(jnp.float32)
    first_step = ((apply_ham(vectors, inner_f, partner, cross_sets) - centre * start_f) / half_span).astype(jnp.bfloat16)
    second_step = (2.0 * (apply_ham(first_step, inner_f, partner, cross_sets) - centre * first_step.astype(jnp.float32)) / half_span - start_f).astype(jnp.bfloat16)
    filtered = (2.0 * (apply_ham(second_step, inner_f, partner, cross_sets) - centre * second_step.astype(jnp.float32)) / half_span - first_step.astype(jnp.float32)).astype(jnp.bfloat16)
    image_next = ((apply_ham(filtered, inner_f, partner, cross_sets) - centre * filtered.astype(jnp.float32)) / half_span).astype(jnp.bfloat16)
    filtered_f = filtered.astype(jnp.float32)
    image_f = image_next.astype(jnp.float32)
    divisor = float(ORB * ATOMS)
    correlation = jnp.einsum('ova,owa->vw', filtered_f, filtered_f) / divisor
    projected = jnp.einsum('ova,owa->vw', image_f, filtered_f) / divisor
    return filtered, correlation, projected
```

```python
import functools

import jax
import jax.numpy as jnp
from jax import lax
from jax.experimental import pallas as pl
from jax.experimental.pallas import tpu as pltpu
from jax.sharding import PartitionSpec as P

MESH = pl.DeviceIdType.MESH
F32 = jnp.float32
BF16 = jnp.bfloat16
ORB = 13
VEC = 64
ATOMS = 128
SLOTS = 6
REACH = 4
EDGE = 16
WIDE = ORB * ATOMS
NZ = 16
NY = 4
HALF_A = 7


def strip_place(orbital, strip):
    return orbital // 8, ((4 + strip + orbital) % 8) * EDGE


def nt_dot(left, right):
    return lax.dot_general(left, right, (((1,), (1,)), ((), ())), preferred_element_type=F32)


def joined(ref, first, last):
    return jnp.concatenate([ref[o] for o in range(first, last)], axis=1)


def kernel(
    vec_in, pairs_in, count_in, blocks_in, cx_in, cy_in, top_ref, cut_ref,
    filt_out, corr_out, proj_out,
    field, pairs, count, blocks, cross, spread, gathered_rows, mask, inner, rim, rim_got,
    strips, strips_got, total, right_side, prev_got, next_got, far_got,
    ysend, ygot, zsend, zgot,
    load_sem, store_sem, rim_send, rim_recv, strip_send, strip_recv, ring_send, ring_recv,
    pair_send, pair_recv, y_send, y_recv, z_send, z_recv,
):
    dx, dy, band = lax.axis_index("dx"), lax.axis_index("dy"), lax.axis_index("band")
    chip, core = band // 2, band % 2
    east = ((dx + 1) % NZ, dy, band)
    west = ((dx + NZ - 1) % NZ, dy, band)
    north = (dx, (dy + 1) % NY, band)
    south = (dx, (dy + NY - 1) % NY, band)
    sibling = (dx, dy, 2 * chip + 1 - core)
    after = (dx, dy, 2 * ((chip + 1) % 4) + core)
    before = (dx, dy, 2 * ((chip + 3) % 4) + core)

    loads = [
        pltpu.make_async_copy(source, target, load_sem.at[index])
        for index, (source, target) in enumerate(
            (
                (vec_in, field.at[0]),
                (cx_in, cross.at[0]),
                (cy_in, cross.at[1]),
                (pairs_in, pairs),
                (count_in, count),
                (blocks_in, blocks),
            )
        )
    ]
    for load in loads:
        load.start()

    barrier = pltpu.get_barrier_semaphore()

    def greet(step, carry):
        pl.semaphore_signal(barrier, inc=1, device_id=((dx + step) % NZ, dy, band), device_id_type=MESH)
        return carry

    lax.fori_loop(1, NZ, greet, 0)
    for dj in range(NY):
        for dk in range(2):
            if dj or dk:
                pl.semaphore_signal(
                    barrier, inc=1,
                    device_id=(dx, (dy + dj) % NY, 2 * chip + (core + dk) % 2), device_id_type=MESH,
                )
    pl.semaphore_signal(barrier, inc=1, device_id=after, device_id_type=MESH)
    pl.semaphore_signal(barrier, inc=1, device_id=before, device_id_type=MESH)

    lane_group = lax.broadcasted_iota(jnp.int32, (VEC, ATOMS), 1) // EDGE

    def send_strips(step):
        for tile, (first, last) in enumerate(((0, 8), (8, ORB))):
            packed = [jnp.zeros((VEC, ATOMS), F32) for _ in range(4)]
            for o in range(first, last):
                turned = field[step, o].astype(F32)
                if o % 8:
                    turned = pltpu.roll(turned, EDGE * (o % 8), 1)
                for s in range(4):
                    packed[s] = jnp.where(lane_group == (4 + s + o) % 8, turned, packed[s])
            for s in range(4):
                strips[step, s, :, tile * ATOMS : (tile + 1) * ATOMS] = packed[s].astype(BF16)

    def strip_copies(step):
        return [
            pltpu.make_async_remote_copy(
                src_ref=strips.at[step, s], dst_ref=strips_got.at[step, s],
                send_sem=strip_send.at[step, s], recv_sem=strip_recv.at[step, s],
                device_id=target, device_id_type=MESH,
            )
            for s, target in enumerate((west, east, south, north))
        ]

    loads[0].wait()
    send_strips(0)

    loads[1].wait()
    loads[2].wait()
    spread[...] = jnp.zeros_like(spread)
    rim[...] = jnp.zeros_like(rim)
    edge_group = lax.broadcasted_iota(jnp.int32, (EDGE, ATOMS), 1) // EDGE
    edge_place = lax.broadcasted_iota(jnp.int32, (EDGE, ATOMS), 1) % EDGE
    edge_row = lax.broadcasted_iota(jnp.int32, (EDGE, ATOMS), 0)
    for axis in range(2):
        row_strip, col_strip = 2 * axis, 2 * axis + 1

        def spread_one(m, carry):
            for o in range(ORB):
                spread[o, 0:ORB, 0:EDGE] = cross[axis, m, o].astype(F32)
            for tile, (first, last) in enumerate(((0, 8), (8, ORB))):
                rows = jnp.zeros((EDGE, ATOMS), F32)
                for o in range(first, last):
                    _, lane = strip_place(o, col_strip)
                    turned = spread[o]
                    if lane:
                        turned = pltpu.roll(turned, lane, 1)
                    rows = jnp.where(edge_group == lane // EDGE, turned, rows)
                gathered_rows[m, :, tile * ATOMS : (tile + 1) * ATOMS] = rows
            return carry

        lax.fori_loop(0, REACH, spread_one, 0)
        for p in range(ORB):
            tile_row, lane_row = strip_place(p, row_strip)
            base = tile_row * ATOMS + lane_row
            for tile in range(2):
                block = jnp.zeros((EDGE, ATOMS), F32)
                for m in range(REACH):
                    line = gathered_rows[m, p : p + 1, tile * ATOMS : (tile + 1) * ATOMS]
                    block = jnp.where((edge_place + m) % EDGE == edge_row, line, block)
                rim[axis, base : base + EDGE, tile * ATOMS : (tile + 1) * ATOMS] = block.astype(BF16)

    pl.semaphore_wait(barrier, NZ - 1 + 2 * NY - 1 + 2)
    for copy in strip_copies(0):
        copy.start()
    rim_copies = [
        pltpu.make_async_remote_copy(
            src_ref=rim.at[axis], dst_ref=rim_got.at[axis],
            send_sem=rim_send.at[axis], recv_sem=rim_recv.at[axis],
            device_id=target, device_id_type=MESH,
        )
        for axis, target in enumerate((east, north))
    ]
    for copy in rim_copies:
        copy.start()

    for load in loads[3:]:
        load.wait()
    partner = lax.broadcasted_iota(jnp.int32, (ATOMS, ATOMS), 0)
    for k in range(SLOTS):
        chosen = jnp.where(k < count[...].reshape(1, ATOMS), pairs[k : k + 1, :], -1)
        mask[k] = jnp.where(partner == chosen, 1.0, 0.0).astype(BF16)

    def build(o, carry):
        for p in range(ORB):
            tile = mask[0] * blocks[0, o, p : p + 1, :]
            for k in range(1, SLOTS):
                tile = tile + mask[k] * blocks[k, o, p : p + 1, :]
            inner[p * ATOMS : (p + 1) * ATOMS, pl.ds(pl.multiple_of(o * ATOMS, ATOMS), ATOMS)] = tile
        return carry

    lax.fori_loop(0, ORB, build, 0)

    half = (jnp.full((1, ATOMS), top_ref[0], F32) - cut_ref[0]) * 0.5
    centre = (top_ref[0] + cut_ref[0]) * 0.5
    inverse = 1.0 / half
    upper = lane_group >= 4

    def interior(step):
        left = joined(field.at[step], 0, ORB)
        for g in range(7):
            first, last = 2 * g, min(2 * g + 2, ORB)
            part = jnp.dot(left, inner[:, first * ATOMS : last * ATOMS], preferred_element_type=F32)
            part = part + nt_dot(left, inner[first * ATOMS : last * ATOMS, :])
            for o in range(first, last):
                total[o] = part[:, (o - first) * ATOMS : (o - first + 1) * ATOMS]

    def finish(step, scale, keep):
        got = strips_got.at[step]
        from_east = jnp.dot(got[0], rim[0], preferred_element_type=F32)
        from_west = nt_dot(got[1], rim_got[0])
        from_north = jnp.dot(got[2], rim[1], preferred_element_type=F32)
        from_south = nt_dot(got[3], rim_got[1])
        added = (from_west, from_east, from_south, from_north)
        for o in range(ORB):
            tile = o // 8
            rows = jnp.zeros((VEC, ATOMS), F32)
            for s in range(4):
                rows = jnp.where(
                    lane_group == (4 + s + o) % 8, added[s][:, tile * ATOMS : (tile + 1) * ATOMS], rows
                )
            if o % 8:
                rows = pltpu.roll(rows, ATOMS - EDGE * (o % 8), 1)
            applied = total[o] + jnp.where(upper, rows, 0.0)
            result = (applied - centre * field[step, o].astype(F32)) * scale
            if keep is not None:
                result = result - field[keep, o].astype(F32)
            field[step + 1, o] = result.astype(BF16)

    own_rows = pl.ds(pl.multiple_of(core * 2 * VEC, 2 * VEC), VEC)
    own_image_rows = pl.ds(pl.multiple_of(core * 2 * VEC + VEC, VEC), VEC)

    def remote(source, target, send, recv, device):
        return pltpu.make_async_remote_copy(
            src_ref=source, dst_ref=target, send_sem=send, recv_sem=recv, device_id=device, device_id_type=MESH
        )

    part_a, part_b = pl.ds(0, HALF_A), pl.ds(HALF_A, ORB - HALF_A)
    ring_copies = [
        remote(field.at[3, part_a], prev_got.at[part_a], ring_send.at[0], ring_recv.at[0], after),
        remote(field.at[3, part_b], next_got.at[part_b], ring_send.at[1], ring_recv.at[1], before),
        remote(field.at[3, part_b], prev_got.at[part_b], ring_send.at[2], ring_recv.at[2], after),
        remote(field.at[3, part_a], next_got.at[part_a], ring_send.at[3], ring_recv.at[3], before),
        remote(prev_got.at[part_a], far_got.at[part_a], ring_send.at[4], ring_recv.at[4], after),
        remote(next_got.at[part_b], far_got.at[part_b], ring_send.at[5], ring_recv.at[5], before),
    ]
    pair_copies = [
        remote(field.at[3], right_side.at[:, own_rows], pair_send.at[0], pair_recv.at[0], sibling),
        remote(field.at[4], right_side.at[:, own_image_rows], pair_send.at[1], pair_recv.at[1], sibling),
    ]
    store = pltpu.make_async_copy(field.at[3], filt_out, store_sem)

    for step in range(4):
        if step:
            send_strips(step)
            for copy in strip_copies(step):
                copy.start()
        if step == 3:
            for copy in ring_copies[:4]:
                copy.start()
            pair_copies[0].start()
            store.start()
        interior(step)
        if step == 0:
            for copy in rim_copies:
                copy.wait_recv()
        if step == 3:
            ring_copies[0].wait_recv()
            ring_copies[4].start()
            ring_copies[1].wait_recv()
            ring_copies[5].start()
        for copy in strip_copies(step):
            copy.wait_recv()
        finish(step, inverse if step in (0, 3) else 2.0 * inverse, {1: 0, 2: 1}.get(step))

    pair_copies[1].start()
    for o in range(ORB):
        right_side[o, own_rows, :] = field[3, o]
        right_side[o, own_image_rows, :] = field[4, o]
    for copy in pair_copies:
        copy.wait_recv()

    def products(ref, offset):
        left = joined(ref, 0, ORB)
        right = joined(right_side, 0, ORB)
        result = nt_dot(left, right)
        rows = pl.ds(pl.multiple_of(((chip + offset) % 4) * 16, 16), 16)
        for j in range(NY):
            for k in range(2):
                lanes = slice(k * ATOMS, (k + 1) * ATOMS)
                piece = jnp.concatenate(
                    [result[8 * j : 8 * j + 8, lanes], result[32 + 8 * j : 40 + 8 * j, lanes]], axis=0
                )
                ysend[j, k, rows, :] = piece.astype(BF16)

    products(field.at[3], 0)
    ring_copies[2].wait_recv()
    products(prev_got, 3)
    ring_copies[3].wait_recv()
    products(next_got, 1)
    ring_copies[4].wait_recv()
    ring_copies[5].wait_recv()
    products(far_got, 2)

    y_copies = {}
    for dj, dk in ((2, 0), (2, 1), (1, 0), (3, 0), (1, 1), (3, 1), (0, 1)):
        to_y, to_core = (dy + dj) % NY, (core + dk) % 2
        slot = 2 * dj + dk
        y_copies[dj, dk] = remote(
            ysend.at[to_y, to_core], ygot.at[slot], y_send.at[slot], y_recv.at[slot],
            (dx, to_y, 2 * chip + to_core),
        )
        y_copies[dj, dk].start()
    for dk in range(2):
        summed = None
        for dj in (0, 1, 3, 2):
            if dj or dk:
                y_copies[dj, dk].wait_recv()
                term = ygot[2 * dj + dk].astype(F32)
            else:
                term = ysend[dy, core].astype(F32)
            summed = term if summed is None else summed + term
        from_core = (core + dk) % 2
        for c in range(4):
            for q in range(2):
                zsend[4 * c + 2 * from_core + q] = summed[16 * c + 8 * q : 16 * c + 8 * q + 8, :]

    def z_copy(step):
        target = (dx + step) % NZ
        return remote(zsend.at[target], zgot.at[step], z_send.at[step], z_recv.at[step], (target, dy, band))

    def z_start(step, carry):
        z_copy(step).start()
        return carry

    lax.fori_loop(1, NZ, z_start, 0)

    def z_take(step, value):
        z_copy(step).wait_recv()
        return value + zgot[step]

    final = lax.fori_loop(1, NZ, z_take, zsend[dx]) * (1.0 / (ORB * ATOMS * NZ * NY))
    turned = jnp.transpose(final)
    corr_out[...] = turned[0:VEC, :]
    proj_out[...] = turned[VEC:, :]

    def z_end(step, carry):
        z_copy(step).wait_send()
        return carry

    lax.fori_loop(1, NZ, z_end, 0)
    for step in range(4):
        for copy in strip_copies(step):
            copy.wait_send()
    for copy in rim_copies + ring_copies + pair_copies + list(y_copies.values()):
        copy.wait_send()
    store.wait()


def on_device(vectors, inner_pairs, inner_count, inner_blocks, cross_x_blocks, cross_y_blocks, spectrum_top, filter_cut):
    any_spec = pl.BlockSpec(memory_space=pl.ANY)
    vmem_spec = pl.BlockSpec(memory_space=pltpu.VMEM)
    smem_spec = pl.BlockSpec(memory_space=pltpu.SMEM)
    dma = pltpu.SemaphoreType.DMA
    small = jax.ShapeDtypeStruct((VEC, 8), F32)
    return pl.pallas_call(
        kernel,
        out_shape=(jax.ShapeDtypeStruct((ORB, VEC, ATOMS), BF16), small, small),
        in_specs=[any_spec] * 6 + [smem_spec] * 2,
        out_specs=(any_spec, vmem_spec, vmem_spec),
        scratch_shapes=[
            pltpu.VMEM((5, ORB, VEC, ATOMS), BF16),
            pltpu.VMEM((SLOTS, ATOMS), jnp.int32),
            pltpu.VMEM((ATOMS,), jnp.int32),
            pltpu.VMEM((SLOTS, ORB, ORB, ATOMS), BF16),
            pltpu.VMEM((2, REACH, ORB, ORB, EDGE), BF16),
            pltpu.VMEM((ORB, EDGE, ATOMS), F32),
            pltpu.VMEM((REACH, EDGE, 2 * ATOMS), F32),
            pltpu.VMEM((SLOTS, ATOMS, ATOMS), BF16),
            pltpu.VMEM((WIDE, WIDE), BF16),
            pltpu.VMEM((2, 2 * ATOMS, 2 * ATOMS), BF16),
            pltpu.VMEM((2, 2 * ATOMS, 2 * ATOMS), BF16),
            pltpu.VMEM((4, 4, VEC, 2 * ATOMS), BF16),
            pltpu.VMEM((4, 4, VEC, 2 * ATOMS), BF16),
            pltpu.VMEM((ORB, VEC, ATOMS), F32),
            pltpu.VMEM((ORB, 4 * VEC, ATOMS), BF16),
            pltpu.VMEM((ORB, VEC, ATOMS), BF16),
            pltpu.VMEM((ORB, VEC, ATOMS), BF16),
            pltpu.VMEM((ORB, VEC, ATOMS), BF16),
            pltpu.VMEM((NY, 2, VEC, ATOMS), BF16),
            pltpu.VMEM((2 * NY, VEC, ATOMS), BF16),
            pltpu.VMEM((NZ, 8, ATOMS), F32),
            pltpu.VMEM((NZ, 8, ATOMS), F32),
            dma((6,)), dma(()), dma((2,)), dma((2,)), dma((4, 4)), dma((4, 4)), dma((6,)), dma((6,)),
            dma((2,)), dma((2,)), dma((2 * NY,)), dma((2 * NY,)), dma((NZ,)), dma((NZ,)),
        ],
        compiler_params=pltpu.CompilerParams(
            collective_id=0, has_side_effects=True, vmem_limit_bytes=48 * 1024 * 1024
        ),
        name="chebyshev",
    )(vectors, inner_pairs, inner_count, inner_blocks, cross_x_blocks, cross_y_blocks, spectrum_top, filter_cut)


def solution(mesh):
    in_specs = (
        P(None, "band", ("dx", "dy")),
        P(None, ("dx", "dy")),
        P(("dx", "dy")),
        P(None, None, None, ("dx", "dy")),
        P(None, None, None, ("dx", "dy")),
        P(None, None, None, ("dx", "dy")),
        P(),
        P(),
    )
    out_specs = (P(None, "band", ("dx", "dy")), P("band", ("dx", "dy")), P("band", ("dx", "dy")))
    return jax.shard_map(on_device, mesh=mesh, in_specs=in_specs, out_specs=out_specs, check_vma=False)
```

```python
import functools

import jax
import jax.numpy as jnp
from jax import lax
from jax.experimental import pallas as pl
from jax.experimental.pallas import tpu as pltpu
from jax.sharding import PartitionSpec as P

MESH = pl.DeviceIdType.MESH
F32 = jnp.float32
BF16 = jnp.bfloat16
ORB = 13
VEC = 64
ATOMS = 128
SLOTS = 6
REACH = 4
EDGE = 16
WIDE = ORB * ATOMS
NZ = 16
VMEM_BYTES = 56 * 1024 * 1024
NY = 4


def nt_dot(left, right):
    return lax.dot_general(left, right, (((1,), (1,)), ((), ())), preferred_element_type=F32)


def joined(ref, first, last):
    return jnp.concatenate([ref[o] for o in range(first, last)], axis=1)


def kernel(
    vec_in, pairs_in, count_in, blocks_in, cx_in, cy_in, top_ref, cut_ref,
    filt_out, sums_out,
    field, pairs, count, blocks, cross, spread, chosen, double, lines, inner, whole, rim, rim_got, rim_lines, rim_sent, rim_came,
    strips, strips_got, total, inside, added, right_side, prev_got, next_got, far_got,
    ysend, ygot, zsend, zgot,
    load_sem, store_sem, rim_send, rim_recv, strip_send, strip_recv, ring_send, ring_recv,
    pair_send, pair_recv, y_send, y_recv, z_send, z_recv,
):
    dx, dy, band = lax.axis_index("dx"), lax.axis_index("dy"), lax.axis_index("band")
    chip, core = band // 2, band % 2
    east = ((dx + 1) % NZ, dy, band)
    west = ((dx + NZ - 1) % NZ, dy, band)
    north = (dx, (dy + 1) % NY, band)
    south = (dx, (dy + NY - 1) % NY, band)
    sibling = (dx, dy, 2 * chip + 1 - core)
    after = (dx, dy, 2 * ((chip + 1) % 4) + core)
    before = (dx, dy, 2 * ((chip + 3) % 4) + core)

    loads = [
        pltpu.make_async_copy(source, target, load_sem.at[index])
        for index, (source, target) in enumerate(
            (
                (vec_in, field.at[0]),
                (cx_in, cross.at[0]),
                (cy_in, cross.at[1]),
                (pairs_in, pairs),
                (count_in, count),
                (blocks_in, blocks),
            )
        )
    ]
    for load in loads:
        load.start()

    barrier = pltpu.get_barrier_semaphore()

    def greet(step, carry):
        pl.semaphore_signal(barrier, inc=1, device_id=((dx + step) % NZ, dy, band), device_id_type=MESH)
        return carry

    lax.fori_loop(1, NZ, greet, 0)
    for dj in range(NY):
        for dk in range(2):
            if dj or dk:
                pl.semaphore_signal(
                    barrier, inc=1,
                    device_id=(dx, (dy + dj) % NY, 2 * chip + (core + dk) % 2), device_id_type=MESH,
                )
    pl.semaphore_signal(barrier, inc=1, device_id=after, device_id_type=MESH)
    pl.semaphore_signal(barrier, inc=1, device_id=before, device_id_type=MESH)

    lane_group = lax.broadcasted_iota(jnp.int32, (VEC, ATOMS), 1) // EDGE

    def pack(source, target):
        for tile, (first, last) in enumerate(((0, 8), (8, ORB))):
            packed = [jnp.zeros((VEC, ATOMS), F32) for _ in range(4)]
            for o in range(first, last):
                turned = source[o].astype(F32)
                if o % 8:
                    turned = pltpu.roll(turned, EDGE * (o % 8), 1)
                for s in range(4):
                    packed[s] = jnp.where(lane_group == (4 + s + o) % 8, turned, packed[s])
            for s in range(4):
                target[s, :, tile * ATOMS : (tile + 1) * ATOMS] = packed[s].astype(target.dtype)

    def strip_copies(step):
        return [
            pltpu.make_async_remote_copy(
                src_ref=strips.at[step, s], dst_ref=strips_got.at[step, s],
                send_sem=strip_send.at[step, s], recv_sem=strip_recv.at[step, s],
                device_id=target, device_id_type=MESH,
            )
            for s, target in enumerate((west, east, south, north))
        ]

    loads[0].wait()
    pack(field.at[0], strips.at[0])

    loads[1].wait()
    loads[2].wait()
    spread[...] = jnp.zeros_like(spread)
    rim[...] = jnp.zeros_like(rim)
    rim_got[...] = jnp.zeros_like(rim_got)
    rim_lines[...] = jnp.zeros_like(rim_lines)
    line_group = lax.broadcasted_iota(jnp.int32, (8, ATOMS), 1) // EDGE
    edge_place = lax.broadcasted_iota(jnp.int32, (EDGE, ATOMS), 1) % EDGE
    edge_row = lax.broadcasted_iota(jnp.int32, (EDGE, ATOMS), 0)
    edge_hits = [(edge_place + m) % EDGE == edge_row for m in range(REACH)]
    for axis in range(2):
        col_strip = 2 * axis + 1

        spread[:, :, 0:REACH, 0:EDGE] = cross[axis].astype(F32)
        for p in range(ORB):
            for tile, (first, last) in enumerate(((0, 8), (8, ORB))):
                packed = jnp.zeros((8, ATOMS), F32)
                for o in range(first, last):
                    group = (4 + col_strip + o) % 8
                    turned = spread[o, p]
                    if group:
                        turned = pltpu.roll(turned, group * EDGE, 1)
                    packed = jnp.where(line_group == group, turned, packed)
                rim_lines[axis, REACH * p : REACH * (p + 1), tile * ATOMS : (tile + 1) * ATOMS] = packed[0:REACH, :]
        rim_sent[axis] = rim_lines[axis].astype(BF16)

    def widen(axis, target):
        for p in range(ORB):
            place = (p // 8) * ATOMS + ((4 + 2 * axis + p) % 8) * EDGE
            for tile in range(2):
                lanes = slice(tile * ATOMS, (tile + 1) * ATOMS)
                block = jnp.zeros((EDGE, ATOMS), F32)
                for m in range(REACH):
                    line = REACH * p + m
                    block = jnp.where(edge_hits[m], rim_lines[axis, line : line + 1, lanes], block)
                target[axis, place : place + EDGE, lanes] = block.astype(BF16)

    for load in loads[3:]:
        load.wait()
    taken = []
    for k in range(SLOTS):
        here = jnp.where(k < count[...].reshape(1, ATOMS), pairs[k : k + 1, :], -1)
        seen = jnp.zeros((1, ATOMS), F32)
        for earlier in range(k):
            same = jnp.where((taken[earlier] == here) & (here >= 0), 1.0, 0.0)
            double[k, earlier : earlier + 1, :] = same
            seen = seen + same
        taken.append(jnp.where(seen > 0.5, -1, here))
        chosen[k : k + 1, :] = taken[k]
    partner = lax.broadcasted_iota(jnp.int32, (EDGE, ATOMS), 0)

    def build(o, carry):
        merged = [blocks[k, o].astype(F32) for k in range(SLOTS)]
        for k in range(1, SLOTS):
            for earlier in range(k):
                merged[earlier] = merged[earlier] + merged[k] * double[k, earlier : earlier + 1, :]
        for k in range(SLOTS):
            lines[k, 0:ORB, :] = merged[k]
        columns = pl.ds(pl.multiple_of(o * ATOMS, ATOMS), ATOMS)
        for start in range(0, ATOMS, EDGE):
            hits = [partner + start == chosen[k : k + 1, :] for k in range(SLOTS)]
            for p in range(ORB):
                piece = jnp.zeros((EDGE, ATOMS), F32)
                for k in range(SLOTS):
                    piece = jnp.where(hits[k], lines[k, p : p + 1, :], piece)
                inner[p * ATOMS + start : p * ATOMS + start + EDGE, columns] = piece.astype(BF16)
        return carry

    lax.fori_loop(0, 7, build, 0)
    pl.semaphore_wait(barrier, NZ - 1 + 2 * NY - 1 + 2)
    rim_copies = [
        pltpu.make_async_remote_copy(
            src_ref=rim_sent.at[axis], dst_ref=rim_came.at[axis],
            send_sem=rim_send.at[axis], recv_sem=rim_recv.at[axis],
            device_id=target, device_id_type=MESH,
        )
        for axis, target in enumerate((east, north))
    ]
    for copy in rim_copies:
        copy.start()
    for copy in strip_copies(0):
        copy.start()
    for axis in range(2):
        widen(axis, rim)
    lax.fori_loop(7, ORB, build, 0)

    half = (jnp.full((1, ATOMS), top_ref[0], F32) - cut_ref[0]) * 0.5
    centre = (top_ref[0] + cut_ref[0]) * 0.5
    inverse = 1.0 / half
    wide_centre = jnp.full((1, 2 * ATOMS), centre, F32)
    wide_inverse = jnp.concatenate([inverse, inverse], axis=1)
    upper = lane_group >= 4

    def interior(step):
        left = joined(field.at[step], 0, ORB)
        for g in range(7):
            first, last = 2 * g, min(2 * g + 2, ORB)
            lanes = slice(first * ATOMS, last * ATOMS)
            if step == 0:
                for q in range(ORB):
                    rows = slice(q * ATOMS, (q + 1) * ATOMS)
                    whole[rows, lanes] = inner[rows, lanes] + jnp.transpose(inner[lanes, rows])
            part = jnp.dot(left, whole[:, lanes], preferred_element_type=F32)
            for o in range(first, last):
                total[o] = part[:, (o - first) * ATOMS : (o - first + 1) * ATOMS]

    def advance(step, s, scale, keep):
        source = (1, 0, 3, 2)[s]
        strip_copies(step)[source].wait_recv()
        got = strips_got[step, source]
        across = (
            jnp.dot(got, rim[s // 2], preferred_element_type=F32) if s % 2 else nt_dot(got, rim_got[s // 2])
        )
        added[s] = across
        if step < 3:
            result = (inside[s] + across - wide_centre * strips[step, s].astype(F32)) * scale
            if keep is not None:
                result = result - strips[keep, s].astype(F32)
            strips[step + 1, s] = result.astype(BF16)
            strip_copies(step + 1)[s].start()

    def finish(step, scale, keep):
        for o in range(ORB):
            tile = o // 8
            rows = jnp.zeros((VEC, ATOMS), F32)
            for s in range(4):
                rows = jnp.where(
                    lane_group == (4 + s + o) % 8, added[s, :, tile * ATOMS : (tile + 1) * ATOMS], rows
                )
            if o % 8:
                rows = pltpu.roll(rows, ATOMS - EDGE * (o % 8), 1)
            applied = total[o] + jnp.where(upper, rows, 0.0)
            result = (applied - centre * field[step, o].astype(F32)) * scale
            if keep is not None:
                result = result - field[keep, o].astype(F32)
            field[step + 1, o] = result.astype(BF16)

    own_rows = pl.ds(pl.multiple_of(core * 2 * VEC, 2 * VEC), VEC)
    own_image_rows = pl.ds(pl.multiple_of(core * 2 * VEC + VEC, VEC), VEC)

    def remote(source, target, send, recv, device):
        return pltpu.make_async_remote_copy(
            src_ref=source, dst_ref=target, send_sem=send, recv_sem=recv, device_id=device, device_id_type=MESH
        )

    def ring_copy(index, source, target, first, last, device):
        part = pl.ds(first, last - first)
        return remote(source.at[part], target.at[part], ring_send.at[index], ring_recv.at[index], device)

    mine = field.at[3]
    ring_copies = [
        ring_copy(0, mine, prev_got, 0, 4, after),
        ring_copy(1, mine, next_got, 7, 10, before),
        ring_copy(2, mine, prev_got, 4, 7, after),
        ring_copy(3, mine, next_got, 10, 13, before),
        ring_copy(4, mine, prev_got, 7, 13, after),
        ring_copy(5, mine, next_got, 0, 7, before),
    ]
    passed_on = [
        ring_copy(6, prev_got, far_got, 0, 4, after),
        ring_copy(7, next_got, far_got, 7, 10, before),
        ring_copy(8, prev_got, far_got, 4, 7, after),
        ring_copy(9, next_got, far_got, 10, 13, before),
    ]

    def pass_on(index):
        ring_copies[index].wait_recv()
        passed_on[index].start()

    pair_copies = [
        remote(field.at[3], right_side.at[:, own_rows], pair_send.at[0], pair_recv.at[0], sibling),
        remote(field.at[4], right_side.at[:, own_image_rows], pair_send.at[1], pair_recv.at[1], sibling),
    ]

    store = pltpu.make_async_copy(field.at[3], filt_out, store_sem)
    for step in range(4):
        keep = {1: 0, 2: 1}.get(step)
        factor = 1.0 if step in (0, 3) else 2.0
        if step == 3:
            for copy in ring_copies:
                copy.start()
            pair_copies[0].start()
            store.start()
        interior(step)
        if step < 3:
            pack(total, inside)
        if step == 0:
            for axis in range(2):
                rim_copies[axis].wait_recv()
                rim_lines[axis] = rim_came[axis].astype(F32)
                widen(axis, rim_got)
        if step == 3:
            pass_on(0)
            pass_on(1)
        for s in range(4):
            advance(step, s, wide_inverse * factor, keep)
        finish(step, inverse * factor, keep)

    pair_copies[1].start()
    pass_on(2)
    pass_on(3)
    for o in range(ORB):
        right_side[o, own_rows, :] = field[3, o]
        right_side[o, own_image_rows, :] = field[4, o]
    for copy in pair_copies:
        copy.wait_recv()

    def products(ref, turn):
        left = joined(ref, 0, ORB)
        right = joined(right_side, 0, ORB)
        result = nt_dot(left, right)
        rows = slice(16 * turn, 16 * turn + 16)
        for j in range(NY):
            for k in range(2):
                lanes = slice(k * ATOMS, (k + 1) * ATOMS)
                piece = jnp.concatenate(
                    [result[8 * j : 8 * j + 8, lanes], result[32 + 8 * j : 40 + 8 * j, lanes]], axis=0
                )
                ysend[j, k, rows, :] = piece.astype(BF16)

    y_copies = []

    def y_start(part, first, last):
        rows = pl.ds(first, last - first)
        for dj, dk in ((2, 0), (2, 1), (1, 0), (3, 0), (1, 1), (3, 1), (0, 1)):
            to_y, to_core = (dy + dj) % NY, (core + dk) % 2
            slot = 2 * dj + dk
            copy = remote(
                ysend.at[to_y, to_core, rows], ygot.at[slot, rows], y_send.at[part, slot], y_recv.at[part, slot],
                (dx, to_y, 2 * chip + to_core),
            )
            copy.start()
            y_copies.append(copy)

    products(field.at[3], 0)
    ring_copies[4].wait_recv()
    products(prev_got, 1)
    ring_copies[5].wait_recv()
    products(next_got, 2)
    y_start(0, 0, 48)
    for copy in passed_on:
        copy.wait_recv()
    products(far_got, 3)
    y_start(1, 48, 64)
    for copy in y_copies:
        copy.wait_recv()
    for dk in range(2):
        summed = ygot[dk].astype(F32) if dk else ysend[dy, core].astype(F32)
        for dj in (1, 3, 2):
            summed = summed + ygot[2 * dj + dk].astype(F32)
        from_core = (core + dk) % 2
        for turn, offset in enumerate((0, 3, 1, 2)):
            for q in range(2):
                place = 4 * ((chip + offset) % 4) + 2 * from_core + q
                zsend[place] = summed[16 * turn + 8 * q : 16 * turn + 8 * q + 8, :]

    def z_copy(step):
        target = (dx + step) % NZ
        return remote(zsend.at[target], zgot.at[step], z_send.at[step], z_recv.at[step], (target, dy, band))

    def z_start(index, carry):
        z_copy(NZ // 2 + (index + 1) // 2 * (1 - 2 * (index % 2))).start()
        return carry

    lax.fori_loop(0, NZ - 1, z_start, 0)

    def z_take(step, value):
        z_copy(step).wait_recv()
        return value + zgot[step]

    final = lax.fori_loop(1, NZ, z_take, zsend[dx]) * (1.0 / (ORB * ATOMS * NZ * NY))
    sums_out[...] = final

    def z_end(step, carry):
        z_copy(step).wait_send()
        return carry

    lax.fori_loop(1, NZ, z_end, 0)
    for step in range(4):
        for copy in strip_copies(step):
            copy.wait_send()
    for copy in rim_copies + ring_copies + passed_on + pair_copies + y_copies:
        copy.wait_send()
    store.wait()


def hand_over(filtered, sums, filt_out, corr_out, proj_out, sem):
    copy = pltpu.make_async_copy(filtered, filt_out, sem)
    copy.start()
    corr_out[...] = sums[:, 0:VEC]
    proj_out[...] = sums[:, VEC:]
    copy.wait()


def on_device(vectors, inner_pairs, inner_count, inner_blocks, cross_x_blocks, cross_y_blocks, spectrum_top, filter_cut):
    any_spec = pl.BlockSpec(memory_space=pl.ANY)
    hbm_spec = pl.BlockSpec(memory_space=pltpu.HBM)
    vmem_spec = pl.BlockSpec(memory_space=pltpu.VMEM)
    smem_spec = pl.BlockSpec(memory_space=pltpu.SMEM)
    dma = pltpu.SemaphoreType.DMA
    block = jax.ShapeDtypeStruct((ORB, VEC, ATOMS), BF16)
    small = jax.ShapeDtypeStruct((8, VEC), F32)
    filtered, sums = pl.pallas_call(
        kernel,
        out_shape=(block, jax.ShapeDtypeStruct((8, ATOMS), F32)),
        in_specs=[hbm_spec] * 6 + [smem_spec] * 2,
        out_specs=(any_spec, vmem_spec),
        scratch_shapes=[
            pltpu.VMEM((5, ORB, VEC, ATOMS), BF16),
            pltpu.VMEM((SLOTS, ATOMS), jnp.int32),
            pltpu.VMEM((ATOMS,), jnp.int32),
            pltpu.VMEM((SLOTS, ORB, ORB, ATOMS), BF16),
            pltpu.VMEM((2, ORB, ORB, REACH, EDGE), BF16),
            pltpu.VMEM((ORB, ORB, 8, ATOMS), F32),
            pltpu.VMEM((8, ATOMS), jnp.int32),
            pltpu.VMEM((SLOTS, 8, ATOMS), F32),
            pltpu.VMEM((SLOTS, EDGE, ATOMS), F32),
            pltpu.VMEM((WIDE, WIDE), BF16),
            pltpu.VMEM((WIDE, WIDE), BF16),
            pltpu.VMEM((2, 2 * ATOMS, 2 * ATOMS), BF16),
            pltpu.VMEM((2, 2 * ATOMS, 2 * ATOMS), BF16),
            pltpu.VMEM((2, VEC, 2 * ATOMS), F32),
            pltpu.VMEM((2, VEC, 2 * ATOMS), BF16),
            pltpu.VMEM((2, VEC, 2 * ATOMS), BF16),
            pltpu.VMEM((4, 4, VEC, 2 * ATOMS), BF16),
            pltpu.VMEM((4, 4, VEC, 2 * ATOMS), BF16),
            pltpu.VMEM((ORB, VEC, ATOMS), F32),
            pltpu.VMEM((4, VEC, 2 * ATOMS), F32),
            pltpu.VMEM((4, VEC, 2 * ATOMS), F32),
            pltpu.VMEM((ORB, 4 * VEC, ATOMS), BF16),
            pltpu.VMEM((ORB, VEC, ATOMS), BF16),
            pltpu.VMEM((ORB, VEC, ATOMS), BF16),
            pltpu.VMEM((ORB, VEC, ATOMS), BF16),
            pltpu.VMEM((NY, 2, VEC, ATOMS), BF16),
            pltpu.VMEM((2 * NY, VEC, ATOMS), BF16),
            pltpu.VMEM((NZ, 8, ATOMS), F32),
            pltpu.VMEM((NZ, 8, ATOMS), F32),
            dma((6,)), dma(()), dma((2,)), dma((2,)), dma((4, 4)), dma((4, 4)), dma((10,)), dma((10,)),
            dma((2,)), dma((2,)), dma((2, 2 * NY)), dma((2, 2 * NY)), dma((NZ,)), dma((NZ,)),
        ],
        compiler_params=pltpu.CompilerParams(
            collective_id=0, has_side_effects=True, vmem_limit_bytes=VMEM_BYTES
        ),
        name="chebyshev",
    )(
        vectors, inner_pairs, inner_count, inner_blocks,
        cross_x_blocks.transpose(1, 2, 0, 3), cross_y_blocks.transpose(1, 2, 0, 3), spectrum_top, filter_cut,
    )
    filtered, correlation, projected = pl.pallas_call(
        hand_over,
        out_shape=(block, small, small),
        in_specs=[vmem_spec, vmem_spec],
        out_specs=(any_spec, vmem_spec, vmem_spec),
        scratch_shapes=[dma(())],
        compiler_params=pltpu.CompilerParams(vmem_limit_bytes=VMEM_BYTES),
        name="hand_over",
    )(filtered, sums)
    return filtered, correlation.T, projected.T


def solution(mesh):
    in_specs = (
        P(None, "band", ("dx", "dy")),
        P(None, ("dx", "dy")),
        P(("dx", "dy")),
        P(None, None, None, ("dx", "dy")),
        P(None, None, None, ("dx", "dy")),
        P(None, None, None, ("dx", "dy")),
        P(),
        P(),
    )
    out_specs = (P(None, "band", ("dx", "dy")), P("band", ("dx", "dy")), P("band", ("dx", "dy")))
    return jax.shard_map(on_device, mesh=mesh, in_specs=in_specs, out_specs=out_specs, check_vma=False)
```

```python
import functools

import jax
import jax.numpy as jnp
from jax import lax
from jax.experimental import pallas as pl
from jax.experimental.pallas import tpu as pltpu
from jax.sharding import PartitionSpec as P

MESH = pl.DeviceIdType.MESH
F32 = jnp.float32
BF16 = jnp.bfloat16
ORB = 13
VEC = 64
ATOMS = 128
SLOTS = 6
REACH = 4
EDGE = 16
WIDE = ORB * ATOMS
NZ = 16
VMEM_BYTES = 56 * 1024 * 1024
NY = 4


def nt_dot(left, right):
    return lax.dot_general(left, right, (((1,), (1,)), ((), ())), preferred_element_type=F32)


def joined(ref, first, last):
    return jnp.concatenate([ref[o] for o in range(first, last)], axis=1)


def kernel(
    vec_in, pairs_in, count_in, blocks_in, cx_in, cy_in, top_in, cut_in,
    filt_out, sums_out,
    field, top_ref, cut_ref, pairs, count, blocks, cross, spread, chosen, double, lines, inner, whole, rim, rim_got, rim_lines, rim_sent, rim_came,
    strips, strips_got, total, inside, added, right_side, prev_got, next_got, far_got,
    ysend, ygot, zsend, zgot,
    load_sem, store_sem, rim_send, rim_recv, strip_send, strip_recv, ring_send, ring_recv,
    pair_send, pair_recv, y_send, y_recv, z_send, z_recv,
):
    dx, dy, band = lax.axis_index("dx"), lax.axis_index("dy"), lax.axis_index("band")
    chip, core = band // 2, band % 2
    east = ((dx + 1) % NZ, dy, band)
    west = ((dx + NZ - 1) % NZ, dy, band)
    north = (dx, (dy + 1) % NY, band)
    south = (dx, (dy + NY - 1) % NY, band)
    sibling = (dx, dy, 2 * chip + 1 - core)
    after = (dx, dy, 2 * ((chip + 1) % 4) + core)
    before = (dx, dy, 2 * ((chip + 3) % 4) + core)

    loads = [
        pltpu.make_async_copy(source, target, load_sem.at[index])
        for index, (source, target) in enumerate(
            (
                (vec_in, field.at[0]),
                (cx_in, cross.at[0]),
                (cy_in, cross.at[1]),
                (pairs_in, pairs),
                (count_in, count),
                (blocks_in, blocks),
                (top_in, top_ref),
                (cut_in, cut_ref),
            )
        )
    ]
    for load in loads:
        load.start()

    barrier = pltpu.get_barrier_semaphore()

    def greet(step, carry):
        pl.semaphore_signal(barrier, inc=1, device_id=((dx + step) % NZ, dy, band), device_id_type=MESH)
        return carry

    lax.fori_loop(1, NZ, greet, 0)
    for dj in range(NY):
        for dk in range(2):
            if dj or dk:
                pl.semaphore_signal(
                    barrier, inc=1,
                    device_id=(dx, (dy + dj) % NY, 2 * chip + (core + dk) % 2), device_id_type=MESH,
                )
    pl.semaphore_signal(barrier, inc=1, device_id=after, device_id_type=MESH)
    pl.semaphore_signal(barrier, inc=1, device_id=before, device_id_type=MESH)

    lane_group = lax.broadcasted_iota(jnp.int32, (VEC, ATOMS), 1) // EDGE

    def pack(source, target):
        for tile, (first, last) in enumerate(((0, 8), (8, ORB))):
            packed = [jnp.zeros((VEC, ATOMS), F32) for _ in range(4)]
            for o in range(first, last):
                turned = source[o].astype(F32)
                if o % 8:
                    turned = pltpu.roll(turned, EDGE * (o % 8), 1)
                for s in range(4):
                    packed[s] = jnp.where(lane_group == (4 + s + o) % 8, turned, packed[s])
            for s in range(4):
                target[s, :, tile * ATOMS : (tile + 1) * ATOMS] = packed[s].astype(target.dtype)

    def strip_copies(step):
        return [
            pltpu.make_async_remote_copy(
                src_ref=strips.at[step, s], dst_ref=strips_got.at[step, s],
                send_sem=strip_send.at[step, s], recv_sem=strip_recv.at[step, s],
                device_id=target, device_id_type=MESH,
            )
            for s, target in enumerate((west, east, south, north))
        ]

    loads[0].wait()
    pack(field.at[0], strips.at[0])

    loads[1].wait()
    loads[2].wait()
    spread[...] = jnp.zeros_like(spread)
    rim[...] = jnp.zeros_like(rim)
    rim_got[...] = jnp.zeros_like(rim_got)
    rim_lines[...] = jnp.zeros_like(rim_lines)
    line_group = lax.broadcasted_iota(jnp.int32, (8, ATOMS), 1) // EDGE
    edge_place = lax.broadcasted_iota(jnp.int32, (EDGE, ATOMS), 1) % EDGE
    edge_row = lax.broadcasted_iota(jnp.int32, (EDGE, ATOMS), 0)
    edge_hits = [(edge_place + m) % EDGE == edge_row for m in range(REACH)]
    for axis in range(2):
        col_strip = 2 * axis + 1

        spread[:, :, 0:REACH, 0:EDGE] = cross[axis].astype(F32)
        for p in range(ORB):
            for tile, (first, last) in enumerate(((0, 8), (8, ORB))):
                packed = jnp.zeros((8, ATOMS), F32)
                for o in range(first, last):
                    group = (4 + col_strip + o) % 8
                    turned = spread[o, p]
                    if group:
                        turned = pltpu.roll(turned, group * EDGE, 1)
                    packed = jnp.where(line_group == group, turned, packed)
                rim_lines[axis, REACH * p : REACH * (p + 1), tile * ATOMS : (tile + 1) * ATOMS] = packed[0:REACH, :]
        rim_sent[axis] = rim_lines[axis].astype(BF16)

    def widen(axis, target):
        for p in range(ORB):
            place = (p // 8) * ATOMS + ((4 + 2 * axis + p) % 8) * EDGE
            for tile in range(2):
                lanes = slice(tile * ATOMS, (tile + 1) * ATOMS)
                block = jnp.zeros((EDGE, ATOMS), F32)
                for m in range(REACH):
                    line = REACH * p + m
                    block = jnp.where(edge_hits[m], rim_lines[axis, line : line + 1, lanes], block)
                target[axis, place : place + EDGE, lanes] = block.astype(BF16)

    for load in loads[3:]:
        load.wait()
    taken = []
    for k in range(SLOTS):
        here = jnp.where(k < count[...].reshape(1, ATOMS), pairs[k : k + 1, :], -1)
        seen = jnp.zeros((1, ATOMS), F32)
        for earlier in range(k):
            same = jnp.where((taken[earlier] == here) & (here >= 0), 1.0, 0.0)
            double[k, earlier : earlier + 1, :] = same
            seen = seen + same
        taken.append(jnp.where(seen > 0.5, -1, here))
        chosen[k : k + 1, :] = taken[k]
    partner = lax.broadcasted_iota(jnp.int32, (EDGE, ATOMS), 0)

    def build(o, carry):
        merged = [blocks[k, o].astype(F32) for k in range(SLOTS)]
        for k in range(1, SLOTS):
            for earlier in range(k):
                merged[earlier] = merged[earlier] + merged[k] * double[k, earlier : earlier + 1, :]
        for k in range(SLOTS):
            lines[k, 0:ORB, :] = merged[k]
        columns = pl.ds(pl.multiple_of(o * ATOMS, ATOMS), ATOMS)
        for start in range(0, ATOMS, EDGE):
            hits = [partner + start == chosen[k : k + 1, :] for k in range(SLOTS)]
            for p in range(ORB):
                piece = jnp.zeros((EDGE, ATOMS), F32)
                for k in range(SLOTS):
                    piece = jnp.where(hits[k], lines[k, p : p + 1, :], piece)
                inner[p * ATOMS + start : p * ATOMS + start + EDGE, columns] = piece.astype(BF16)
        return carry

    lax.fori_loop(0, 7, build, 0)
    pl.semaphore_wait(barrier, NZ - 1 + 2 * NY - 1 + 2)
    rim_copies = [
        pltpu.make_async_remote_copy(
            src_ref=rim_sent.at[axis], dst_ref=rim_came.at[axis],
            send_sem=rim_send.at[axis], recv_sem=rim_recv.at[axis],
            device_id=target, device_id_type=MESH,
        )
        for axis, target in enumerate((east, north))
    ]
    for copy in rim_copies:
        copy.start()
    for copy in strip_copies(0):
        copy.start()
    for axis in range(2):
        widen(axis, rim)
    lax.fori_loop(7, ORB, build, 0)

    half = (jnp.full((1, ATOMS), top_ref[0], F32) - cut_ref[0]) * 0.5
    centre = (top_ref[0] + cut_ref[0]) * 0.5
    inverse = 1.0 / half
    wide_centre = jnp.full((1, 2 * ATOMS), centre, F32)
    wide_inverse = jnp.concatenate([inverse, inverse], axis=1)
    upper = lane_group >= 4

    def interior(step):
        left = joined(field.at[step], 0, ORB)
        for g in range(7):
            first, last = 2 * g, min(2 * g + 2, ORB)
            lanes = slice(first * ATOMS, last * ATOMS)
            if step == 0:
                for q in range(ORB):
                    rows = slice(q * ATOMS, (q + 1) * ATOMS)
                    whole[rows, lanes] = inner[rows, lanes] + jnp.transpose(inner[lanes, rows])
            part = jnp.dot(left, whole[:, lanes], preferred_element_type=F32)
            for o in range(first, last):
                total[o] = part[:, (o - first) * ATOMS : (o - first + 1) * ATOMS]

    def advance(step, s, scale, keep):
        source = (1, 0, 3, 2)[s]
        strip_copies(step)[source].wait_recv()
        got = strips_got[step, source]
        across = (
            jnp.dot(got, rim[s // 2], preferred_element_type=F32) if s % 2 else nt_dot(got, rim_got[s // 2])
        )
        added[s] = across
        if step < 3:
            result = (inside[s] + across - wide_centre * strips[step, s].astype(F32)) * scale
            if keep is not None:
                result = result - strips[keep, s].astype(F32)
            strips[step + 1, s] = result.astype(BF16)
            strip_copies(step + 1)[s].start()

    def finish(step, scale, keep):
        for o in (0, 1, 2, 3, 7, 8, 9, 4, 5, 6, 10, 11, 12):
            tile = o // 8
            rows = jnp.zeros((VEC, ATOMS), F32)
            for s in range(4):
                rows = jnp.where(
                    lane_group == (4 + s + o) % 8, added[s, :, tile * ATOMS : (tile + 1) * ATOMS], rows
                )
            if o % 8:
                rows = pltpu.roll(rows, ATOMS - EDGE * (o % 8), 1)
            applied = total[o] + jnp.where(upper, rows, 0.0)
            result = (applied - centre * field[step, o].astype(F32)) * scale
            if keep is not None:
                result = result - field[keep, o].astype(F32)
            field[step + 1, o] = result.astype(BF16)
            if step == 2:
                for index in {3: (0,), 9: (1,), 6: (2, 5), 12: (3, 4)}.get(o, ()):
                    ring_copies[index].start()

    own_rows = pl.ds(pl.multiple_of(core * 2 * VEC, 2 * VEC), VEC)
    own_image_rows = pl.ds(pl.multiple_of(core * 2 * VEC + VEC, VEC), VEC)

    def remote(source, target, send, recv, device):
        return pltpu.make_async_remote_copy(
            src_ref=source, dst_ref=target, send_sem=send, recv_sem=recv, device_id=device, device_id_type=MESH
        )

    def ring_copy(index, source, target, first, last, device):
        part = pl.ds(first, last - first)
        return remote(source.at[part], target.at[part], ring_send.at[index], ring_recv.at[index], device)

    mine = field.at[3]
    ring_copies = [
        ring_copy(0, mine, prev_got, 0, 4, after),
        ring_copy(1, mine, next_got, 7, 10, before),
        ring_copy(2, mine, prev_got, 4, 7, after),
        ring_copy(3, mine, next_got, 10, 13, before),
        ring_copy(4, mine, prev_got, 7, 13, after),
        ring_copy(5, mine, next_got, 0, 7, before),
    ]
    passed_on = [
        ring_copy(6, prev_got, far_got, 0, 4, after),
        ring_copy(7, next_got, far_got, 7, 10, before),
        ring_copy(8, prev_got, far_got, 4, 7, after),
        ring_copy(9, next_got, far_got, 10, 13, before),
    ]

    def pass_on(index):
        ring_copies[index].wait_recv()
        passed_on[index].start()

    pair_copies = [
        remote(field.at[3], right_side.at[:, own_rows], pair_send.at[0], pair_recv.at[0], sibling),
        remote(field.at[4], right_side.at[:, own_image_rows], pair_send.at[1], pair_recv.at[1], sibling),
    ]

    store = pltpu.make_async_copy(field.at[3], filt_out, store_sem)
    for step in range(4):
        keep = {1: 0, 2: 1}.get(step)
        factor = 1.0 if step in (0, 3) else 2.0
        if step == 3:
            pair_copies[0].start()
            store.start()
        interior(step)
        if step < 3:
            pack(total, inside)
        if step == 0:
            for axis in range(2):
                rim_copies[axis].wait_recv()
                rim_lines[axis] = rim_came[axis].astype(F32)
                widen(axis, rim_got)
        if step == 3:
            pass_on(0)
            pass_on(1)
        for s in range(4):
            advance(step, s, wide_inverse * factor, keep)
        finish(step, inverse * factor, keep)

    pair_copies[1].start()
    pass_on(2)
    pass_on(3)
    for o in range(ORB):
        right_side[o, own_rows, :] = field[3, o]
        right_side[o, own_image_rows, :] = field[4, o]
    for copy in pair_copies:
        copy.wait_recv()

    def products(ref, turn):
        left = joined(ref, 0, ORB)
        right = joined(right_side, 0, ORB)
        result = nt_dot(left, right)
        rows = slice(16 * turn, 16 * turn + 16)
        for j in range(NY):
            for k in range(2):
                lanes = slice(k * ATOMS, (k + 1) * ATOMS)
                piece = jnp.concatenate(
                    [result[8 * j : 8 * j + 8, lanes], result[32 + 8 * j : 40 + 8 * j, lanes]], axis=0
                )
                ysend[j, k, rows, :] = piece.astype(BF16)

    y_copies = []

    def y_start(part, first, last):
        rows = pl.ds(first, last - first)
        for dj, dk in ((2, 0), (2, 1), (1, 0), (3, 0), (1, 1), (3, 1), (0, 1)):
            to_y, to_core = (dy + dj) % NY, (core + dk) % 2
            slot = 2 * dj + dk
            copy = remote(
                ysend.at[to_y, to_core, rows], ygot.at[slot, rows], y_send.at[part, slot], y_recv.at[part, slot],
                (dx, to_y, 2 * chip + to_core),
            )
            copy.start()
            y_copies.append(copy)

    products(field.at[3], 0)
    ring_copies[4].wait_recv()
    products(prev_got, 1)
    ring_copies[5].wait_recv()
    products(next_got, 2)
    y_start(0, 0, 48)
    for copy in passed_on:
        copy.wait_recv()
    products(far_got, 3)
    y_start(1, 48, 64)
    for copy in y_copies:
        copy.wait_recv()
    for dk in range(2):
        summed = ygot[dk].astype(F32) if dk else ysend[dy, core].astype(F32)
        for dj in (1, 3, 2):
            summed = summed + ygot[2 * dj + dk].astype(F32)
        from_core = (core + dk) % 2
        for turn, offset in enumerate((0, 3, 1, 2)):
            for q in range(2):
                place = 4 * ((chip + offset) % 4) + 2 * from_core + q
                zsend[place] = summed[16 * turn + 8 * q : 16 * turn + 8 * q + 8, :]

    def z_copy(step):
        target = (dx + step) % NZ
        return remote(zsend.at[target], zgot.at[step], z_send.at[step], z_recv.at[step], (target, dy, band))

    def z_start(index, carry):
        z_copy(NZ // 2 + (index + 1) // 2 * (1 - 2 * (index % 2))).start()
        return carry

    lax.fori_loop(0, NZ - 1, z_start, 0)

    def z_take(step, value):
        z_copy(step).wait_recv()
        return value + zgot[step]

    final = lax.fori_loop(1, NZ, z_take, zsend[dx]) * (1.0 / (ORB * ATOMS * NZ * NY))
    sums_out[...] = final

    def z_end(step, carry):
        z_copy(step).wait_send()
        return carry

    lax.fori_loop(1, NZ, z_end, 0)
    for step in range(4):
        for copy in strip_copies(step):
            copy.wait_send()
    for copy in rim_copies + ring_copies + passed_on + pair_copies + y_copies:
        copy.wait_send()
    store.wait()


def hand_over(filtered, sums, filt_out, corr_out, proj_out, held, held_sums, corr, proj, load_sem, store_sem):
    parts = [pl.ds(first, last - first) for first, last in ((0, 3), (3, 6), (6, 9), (9, ORB))]
    loads = [
        pltpu.make_async_copy(filtered.at[part], held.at[part], load_sem.at[index]) for index, part in enumerate(parts)
    ]
    stores = [
        pltpu.make_async_copy(held.at[part], filt_out.at[part], store_sem.at[index]) for index, part in enumerate(parts)
    ]
    load_sums = pltpu.make_async_copy(sums, held_sums, load_sem.at[4])
    load_sums.start()
    for load in loads:
        load.start()
    stores.append(pltpu.make_async_copy(corr, corr_out, store_sem.at[4]))
    stores.append(pltpu.make_async_copy(proj, proj_out, store_sem.at[5]))
    load_sums.wait()
    corr[...] = held_sums[:, 0:VEC]
    proj[...] = held_sums[:, VEC:]
    stores[4].start()
    stores[5].start()
    for load, store in zip(loads, stores):
        load.wait()
        store.start()
    for store in stores:
        store.wait()


def on_device(vectors, inner_pairs, inner_count, inner_blocks, cross_x_blocks, cross_y_blocks, spectrum_top, filter_cut):
    any_spec = pl.BlockSpec(memory_space=pl.ANY)
    hbm_spec = pl.BlockSpec(memory_space=pltpu.HBM)
    vmem_spec = pl.BlockSpec(memory_space=pltpu.VMEM)
    dma = pltpu.SemaphoreType.DMA
    block = jax.ShapeDtypeStruct((ORB, VEC, ATOMS), BF16)
    small = jax.ShapeDtypeStruct((8, VEC), F32)
    filtered, sums = pl.pallas_call(
        kernel,
        out_shape=(block, jax.ShapeDtypeStruct((8, ATOMS), F32)),
        in_specs=[hbm_spec] * 8,
        out_specs=(any_spec, vmem_spec),
        scratch_shapes=[
            pltpu.VMEM((5, ORB, VEC, ATOMS), BF16),
            pltpu.SMEM((1,), F32),
            pltpu.SMEM((1,), F32),
            pltpu.VMEM((SLOTS, ATOMS), jnp.int32),
            pltpu.VMEM((ATOMS,), jnp.int32),
            pltpu.VMEM((SLOTS, ORB, ORB, ATOMS), BF16),
            pltpu.VMEM((2, ORB, ORB, REACH, EDGE), BF16),
            pltpu.VMEM((ORB, ORB, 8, ATOMS), F32),
            pltpu.VMEM((8, ATOMS), jnp.int32),
            pltpu.VMEM((SLOTS, 8, ATOMS), F32),
            pltpu.VMEM((SLOTS, EDGE, ATOMS), F32),
            pltpu.VMEM((WIDE, WIDE), BF16),
            pltpu.VMEM((WIDE, WIDE), BF16),
            pltpu.VMEM((2, 2 * ATOMS, 2 * ATOMS), BF16),
            pltpu.VMEM((2, 2 * ATOMS, 2 * ATOMS), BF16),
            pltpu.VMEM((2, VEC, 2 * ATOMS), F32),
            pltpu.VMEM((2, VEC, 2 * ATOMS), BF16),
            pltpu.VMEM((2, VEC, 2 * ATOMS), BF16),
            pltpu.VMEM((4, 4, VEC, 2 * ATOMS), BF16),
            pltpu.VMEM((4, 4, VEC, 2 * ATOMS), BF16),
            pltpu.VMEM((ORB, VEC, ATOMS), F32),
            pltpu.VMEM((4, VEC, 2 * ATOMS), F32),
            pltpu.VMEM((4, VEC, 2 * ATOMS), F32),
            pltpu.VMEM((ORB, 4 * VEC, ATOMS), BF16),
            pltpu.VMEM((ORB, VEC, ATOMS), BF16),
            pltpu.VMEM((ORB, VEC, ATOMS), BF16),
            pltpu.VMEM((ORB, VEC, ATOMS), BF16),
            pltpu.VMEM((NY, 2, VEC, ATOMS), BF16),
            pltpu.VMEM((2 * NY, VEC, ATOMS), BF16),
            pltpu.VMEM((NZ, 8, ATOMS), F32),
            pltpu.VMEM((NZ, 8, ATOMS), F32),
            dma((8,)), dma(()), dma((2,)), dma((2,)), dma((4, 4)), dma((4, 4)), dma((10,)), dma((10,)),
            dma((2,)), dma((2,)), dma((2, 2 * NY)), dma((2, 2 * NY)), dma((NZ,)), dma((NZ,)),
        ],
        compiler_params=pltpu.CompilerParams(
            collective_id=0, has_side_effects=True, vmem_limit_bytes=VMEM_BYTES
        ),
        name="chebyshev",
    )(
        vectors, inner_pairs, inner_count, inner_blocks,
        cross_x_blocks.transpose(1, 2, 0, 3), cross_y_blocks.transpose(1, 2, 0, 3), spectrum_top, filter_cut,
    )
    filtered, correlation, projected = pl.pallas_call(
        hand_over,
        out_shape=(block, small, small),
        in_specs=[any_spec, any_spec],
        out_specs=(any_spec, any_spec, any_spec),
        scratch_shapes=[
            pltpu.VMEM((ORB, VEC, ATOMS), BF16), pltpu.VMEM((8, ATOMS), F32), pltpu.VMEM((8, VEC), F32),
            pltpu.VMEM((8, VEC), F32), dma((5,)), dma((6,)),
        ],
        compiler_params=pltpu.CompilerParams(vmem_limit_bytes=VMEM_BYTES),
        name="hand_over",
    )(filtered, sums)
    return filtered, correlation.T, projected.T


def solution(mesh):
    in_specs = (
        P(None, "band", ("dx", "dy")),
        P(None, ("dx", "dy")),
        P(("dx", "dy")),
        P(None, None, None, ("dx", "dy")),
        P(None, None, None, ("dx", "dy")),
        P(None, None, None, ("dx", "dy")),
        P(),
        P(),
    )
    out_specs = (P(None, "band", ("dx", "dy")), P("band", ("dx", "dy")), P("band", ("dx", "dy")))
    return jax.shard_map(on_device, mesh=mesh, in_specs=in_specs, out_specs=out_specs, check_vma=False)
```

```python
import functools

import jax
import jax.numpy as jnp
from jax import lax
from jax.experimental import pallas as pl
from jax.experimental.pallas import tpu as pltpu
from jax.sharding import PartitionSpec as P

MESH = pl.DeviceIdType.MESH
F32 = jnp.float32
BF16 = jnp.bfloat16
ORB = 13
VEC = 64
ATOMS = 128
SLOTS = 6
REACH = 4
EDGE = 16
WIDE = ORB * ATOMS
NZ = 16
VMEM_BYTES = 56 * 1024 * 1024
NY = 4


def nt_dot(left, right):
    return lax.dot_general(left, right, (((1,), (1,)), ((), ())), preferred_element_type=F32)


def joined(ref, first, last):
    return jnp.concatenate([ref[o] for o in range(first, last)], axis=1)


def kernel(
    vec_in, pairs_in, count_in, blocks_in, cx_in, cy_in, top_in, cut_in,
    filt_out, sums_out,
    field, top_ref, cut_ref, pairs, count, blocks, cross, spread, chosen, double, lines, inner, whole, rim, rim_got, rim_lines, rim_sent, rim_came,
    strips, strips_got, total, inside, added, right_side, prev_got, next_got, far_got,
    ysend, ygot, zsend, zgot,
    load_sem, store_sem, rim_send, rim_recv, strip_send, strip_recv, ring_send, ring_recv,
    pair_send, pair_recv, y_send, y_recv, z_send, z_recv,
):
    dx, dy, band = lax.axis_index("dx"), lax.axis_index("dy"), lax.axis_index("band")
    chip, core = band // 2, band % 2
    east = ((dx + 1) % NZ, dy, band)
    west = ((dx + NZ - 1) % NZ, dy, band)
    north = (dx, (dy + 1) % NY, band)
    south = (dx, (dy + NY - 1) % NY, band)
    sibling = (dx, dy, 2 * chip + 1 - core)
    after = (dx, dy, 2 * ((chip + 1) % 4) + core)
    before = (dx, dy, 2 * ((chip + 3) % 4) + core)

    loads = [
        pltpu.make_async_copy(source, target, load_sem.at[index])
        for index, (source, target) in enumerate(
            (
                (vec_in, field.at[0]),
                (cx_in, cross.at[0]),
                (cy_in, cross.at[1]),
                (pairs_in, pairs),
                (count_in, count),
                (blocks_in, blocks),
                (top_in, top_ref),
                (cut_in, cut_ref),
            )
        )
    ]
    for load in loads:
        load.start()

    barrier = pltpu.get_barrier_semaphore()

    def greet(step, carry):
        pl.semaphore_signal(barrier, inc=1, device_id=((dx + step) % NZ, dy, band), device_id_type=MESH)
        return carry

    lax.fori_loop(1, NZ, greet, 0)
    for dj in range(NY):
        for dk in range(2):
            if dj or dk:
                pl.semaphore_signal(
                    barrier, inc=1,
                    device_id=(dx, (dy + dj) % NY, 2 * chip + (core + dk) % 2), device_id_type=MESH,
                )
    pl.semaphore_signal(barrier, inc=1, device_id=after, device_id_type=MESH)
    pl.semaphore_signal(barrier, inc=1, device_id=before, device_id_type=MESH)

    lane_group = lax.broadcasted_iota(jnp.int32, (VEC, ATOMS), 1) // EDGE

    def pack(source, target):
        for tile, (first, last) in enumerate(((0, 8), (8, ORB))):
            packed = [jnp.zeros((VEC, ATOMS), F32) for _ in range(4)]
            for o in range(first, last):
                turned = source[o].astype(F32)
                if o % 8:
                    turned = pltpu.roll(turned, EDGE * (o % 8), 1)
                for s in range(4):
                    packed[s] = jnp.where(lane_group == (4 + s + o) % 8, turned, packed[s])
            for s in range(4):
                target[s, :, tile * ATOMS : (tile + 1) * ATOMS] = packed[s].astype(target.dtype)

    def strip_copies(step):
        return [
            pltpu.make_async_remote_copy(
                src_ref=strips.at[step, s], dst_ref=strips_got.at[step, s],
                send_sem=strip_send.at[step, s], recv_sem=strip_recv.at[step, s],
                device_id=target, device_id_type=MESH,
            )
            for s, target in enumerate((west, east, south, north))
        ]

    loads[0].wait()
    pack(field.at[0], strips.at[0])

    loads[1].wait()
    loads[2].wait()
    spread[...] = jnp.zeros_like(spread)
    rim[...] = jnp.zeros_like(rim)
    rim_got[...] = jnp.zeros_like(rim_got)
    rim_lines[...] = jnp.zeros_like(rim_lines)
    line_group = lax.broadcasted_iota(jnp.int32, (8, ATOMS), 1) // EDGE
    edge_place = lax.broadcasted_iota(jnp.int32, (EDGE, ATOMS), 1) % EDGE
    edge_row = lax.broadcasted_iota(jnp.int32, (EDGE, ATOMS), 0)
    edge_hits = [(edge_place + m) % EDGE == edge_row for m in range(REACH)]
    for axis in range(2):
        col_strip = 2 * axis + 1

        spread[:, :, 0:REACH, 0:EDGE] = cross[axis].astype(F32)
        for p in range(ORB):
            for tile, (first, last) in enumerate(((0, 8), (8, ORB))):
                packed = jnp.zeros((8, ATOMS), F32)
                for o in range(first, last):
                    group = (4 + col_strip + o) % 8
                    turned = spread[o, p]
                    if group:
                        turned = pltpu.roll(turned, group * EDGE, 1)
                    packed = jnp.where(line_group == group, turned, packed)
                rim_lines[axis, REACH * p : REACH * (p + 1), tile * ATOMS : (tile + 1) * ATOMS] = packed[0:REACH, :]
        rim_sent[axis] = rim_lines[axis].astype(BF16)

    def widen(axis, target):
        for p in range(ORB):
            place = (p // 8) * ATOMS + ((4 + 2 * axis + p) % 8) * EDGE
            for tile in range(2):
                lanes = slice(tile * ATOMS, (tile + 1) * ATOMS)
                block = jnp.zeros((EDGE, ATOMS), F32)
                for m in range(REACH):
                    line = REACH * p + m
                    block = jnp.where(edge_hits[m], rim_lines[axis, line : line + 1, lanes], block)
                target[axis, place : place + EDGE, lanes] = block.astype(BF16)

    for load in loads[3:]:
        load.wait()
    taken = []
    for k in range(SLOTS):
        here = jnp.where(k < count[...].reshape(1, ATOMS), pairs[k : k + 1, :], -1)
        seen = jnp.zeros((1, ATOMS), F32)
        for earlier in range(k):
            same = jnp.where((taken[earlier] == here) & (here >= 0), 1.0, 0.0)
            double[k, earlier : earlier + 1, :] = same
            seen = seen + same
        taken.append(jnp.where(seen > 0.5, -1, here))
        chosen[k : k + 1, :] = taken[k]
    partner = lax.broadcasted_iota(jnp.int32, (EDGE, ATOMS), 0)

    def build(o, carry):
        merged = [blocks[k, o].astype(F32) for k in range(SLOTS)]
        for k in range(1, SLOTS):
            for earlier in range(k):
                merged[earlier] = merged[earlier] + merged[k] * double[k, earlier : earlier + 1, :]
        for k in range(SLOTS):
            lines[k, 0:ORB, :] = merged[k]
        columns = pl.ds(pl.multiple_of(o * ATOMS, ATOMS), ATOMS)
        for start in range(0, ATOMS, EDGE):
            hits = [partner + start == chosen[k : k + 1, :] for k in range(SLOTS)]
            for p in range(ORB):
                piece = jnp.zeros((EDGE, ATOMS), F32)
                for k in range(SLOTS):
                    piece = jnp.where(hits[k], lines[k, p : p + 1, :], piece)
                inner[p * ATOMS + start : p * ATOMS + start + EDGE, columns] = piece.astype(BF16)
        return carry

    lax.fori_loop(0, 7, build, 0)
    pl.semaphore_wait(barrier, NZ - 1 + 2 * NY - 1 + 2)
    rim_copies = [
        pltpu.make_async_remote_copy(
            src_ref=rim_sent.at[axis], dst_ref=rim_came.at[axis],
            send_sem=rim_send.at[axis], recv_sem=rim_recv.at[axis],
            device_id=target, device_id_type=MESH,
        )
        for axis, target in enumerate((east, north))
    ]
    for copy in rim_copies:
        copy.start()
    for copy in strip_copies(0):
        copy.start()
    for axis in range(2):
        widen(axis, rim)
    lax.fori_loop(7, ORB, build, 0)

    half = (jnp.full((1, ATOMS), top_ref[0], F32) - cut_ref[0]) * 0.5
    centre = (top_ref[0] + cut_ref[0]) * 0.5
    inverse = 1.0 / half
    wide_centre = jnp.full((1, 2 * ATOMS), centre, F32)
    wide_inverse = jnp.concatenate([inverse, inverse], axis=1)
    upper = lane_group >= 4

    def interior(step):
        left = joined(field.at[step], 0, ORB)
        for g in range(7):
            first, last = 2 * g, min(2 * g + 2, ORB)
            lanes = slice(first * ATOMS, last * ATOMS)
            if step == 0:
                for q in range(ORB):
                    rows = slice(q * ATOMS, (q + 1) * ATOMS)
                    whole[rows, lanes] = inner[rows, lanes] + jnp.transpose(inner[lanes, rows])
            part = jnp.dot(left, whole[:, lanes], preferred_element_type=F32)
            for o in range(first, last):
                total[o] = part[:, (o - first) * ATOMS : (o - first + 1) * ATOMS]

    def advance(step, s, scale, keep):
        source = (1, 0, 3, 2)[s]
        strip_copies(step)[source].wait_recv()
        got = strips_got[step, source]
        across = (
            jnp.dot(got, rim[s // 2], preferred_element_type=F32) if s % 2 else nt_dot(got, rim_got[s // 2])
        )
        added[s] = across
        if step < 3:
            result = (inside[s] + across - wide_centre * strips[step, s].astype(F32)) * scale
            if keep is not None:
                result = result - strips[keep, s].astype(F32)
            strips[step + 1, s] = result.astype(BF16)
            strip_copies(step + 1)[s].start()

    def finish(step, scale, keep):
        for o in (0, 1, 2, 3, 7, 8, 9, 4, 5, 6, 10, 11, 12):
            tile = o // 8
            rows = jnp.zeros((VEC, ATOMS), F32)
            for s in range(4):
                rows = jnp.where(
                    lane_group == (4 + s + o) % 8, added[s, :, tile * ATOMS : (tile + 1) * ATOMS], rows
                )
            if o % 8:
                rows = pltpu.roll(rows, ATOMS - EDGE * (o % 8), 1)
            applied = total[o] + jnp.where(upper, rows, 0.0)
            result = (applied - centre * field[step, o].astype(F32)) * scale
            if keep is not None:
                result = result - field[keep, o].astype(F32)
            field[step + 1, o] = result.astype(BF16)
            if step == 2:
                for index in {3: (0,), 9: (1,), 6: (2, 5), 12: (3, 4)}.get(o, ()):
                    ring_copies[index].start()

    own_rows = pl.ds(pl.multiple_of(core * 2 * VEC, 2 * VEC), VEC)
    own_image_rows = pl.ds(pl.multiple_of(core * 2 * VEC + VEC, VEC), VEC)

    def remote(source, target, send, recv, device):
        return pltpu.make_async_remote_copy(
            src_ref=source, dst_ref=target, send_sem=send, recv_sem=recv, device_id=device, device_id_type=MESH
        )

    def ring_copy(index, source, target, first, last, device):
        part = pl.ds(first, last - first)
        return remote(source.at[part], target.at[part], ring_send.at[index], ring_recv.at[index], device)

    mine = field.at[3]
    ring_copies = [
        ring_copy(0, mine, prev_got, 0, 4, after),
        ring_copy(1, mine, next_got, 7, 10, before),
        ring_copy(2, mine, prev_got, 4, 7, after),
        ring_copy(3, mine, next_got, 10, 13, before),
        ring_copy(4, mine, prev_got, 7, 13, after),
        ring_copy(5, mine, next_got, 0, 7, before),
    ]
    passed_on = [
        ring_copy(6, prev_got, far_got, 0, 4, after),
        ring_copy(7, next_got, far_got, 7, 10, before),
        ring_copy(8, prev_got, far_got, 4, 7, after),
        ring_copy(9, next_got, far_got, 10, 13, before),
    ]

    def pass_on(index):
        ring_copies[index].wait_recv()
        passed_on[index].start()

    pair_copies = [
        remote(field.at[3], right_side.at[:, own_rows], pair_send.at[0], pair_recv.at[0], sibling),
        remote(field.at[4], right_side.at[:, own_image_rows], pair_send.at[1], pair_recv.at[1], sibling),
    ]

    store = pltpu.make_async_copy(field.at[3], filt_out, store_sem)
    for step in range(4):
        keep = {1: 0, 2: 1}.get(step)
        factor = 1.0 if step in (0, 3) else 2.0
        if step == 3:
            pair_copies[0].start()
            store.start()
        interior(step)
        if step < 3:
            pack(total, inside)
        if step == 0:
            for axis in range(2):
                rim_copies[axis].wait_recv()
                rim_lines[axis] = rim_came[axis].astype(F32)
                widen(axis, rim_got)
        if step == 3:
            pass_on(0)
            pass_on(1)
        for s in range(4):
            advance(step, s, wide_inverse * factor, keep)
        finish(step, inverse * factor, keep)

    pair_copies[1].start()
    pass_on(2)
    pass_on(3)
    for o in range(ORB):
        right_side[o, own_rows, :] = field[3, o]
        right_side[o, own_image_rows, :] = field[4, o]
    for copy in pair_copies:
        copy.wait_recv()

    def products(ref, turn):
        left = joined(ref, 0, ORB)
        right = joined(right_side, 0, ORB)
        result = nt_dot(left, right)
        rows = slice(16 * turn, 16 * turn + 16)
        for j in range(NY):
            for k in range(2):
                lanes = slice(k * ATOMS, (k + 1) * ATOMS)
                piece = jnp.concatenate(
                    [result[8 * j : 8 * j + 8, lanes], result[32 + 8 * j : 40 + 8 * j, lanes]], axis=0
                )
                ysend[j, k, rows, :] = piece.astype(BF16)

    y_copies = []

    def y_start(part, first, last):
        rows = pl.ds(first, last - first)
        for dj, dk in ((2, 0), (2, 1), (1, 0), (3, 0), (1, 1), (3, 1), (0, 1)):
            to_y, to_core = (dy + dj) % NY, (core + dk) % 2
            slot = 2 * dj + dk
            copy = remote(
                ysend.at[to_y, to_core, rows], ygot.at[slot, rows], y_send.at[part, slot], y_recv.at[part, slot],
                (dx, to_y, 2 * chip + to_core),
            )
            copy.start()
            y_copies.append(copy)

    products(field.at[3], 0)
    ring_copies[4].wait_recv()
    products(prev_got, 1)
    ring_copies[5].wait_recv()
    products(next_got, 2)
    y_start(0, 0, 48)
    for copy in passed_on:
        copy.wait_recv()
    products(far_got, 3)
    y_start(1, 48, 64)
    for copy in y_copies:
        copy.wait_recv()
    for dk in range(2):
        summed = ygot[dk].astype(F32) if dk else ysend[dy, core].astype(F32)
        for dj in (1, 3, 2):
            summed = summed + ygot[2 * dj + dk].astype(F32)
        from_core = (core + dk) % 2
        for turn, offset in enumerate((0, 3, 1, 2)):
            for q in range(2):
                place = 4 * ((chip + offset) % 4) + 2 * from_core + q
                zsend[place] = summed[16 * turn + 8 * q : 16 * turn + 8 * q + 8, :]

    def z_copy(step):
        target = (dx + step) % NZ
        return remote(zsend.at[target], zgot.at[step], z_send.at[step], z_recv.at[step], (target, dy, band))

    def z_start(index, carry):
        z_copy(NZ // 2 + (index + 1) // 2 * (1 - 2 * (index % 2))).start()
        return carry

    lax.fori_loop(0, NZ - 1, z_start, 0)

    def z_end(step, carry):
        z_copy(step).wait_send()
        return carry

    lax.fori_loop(1, NZ, z_end, 0)
    for step in range(4):
        for copy in strip_copies(step):
            copy.wait_send()
    for copy in rim_copies + ring_copies + passed_on + pair_copies + y_copies:
        copy.wait_send()
    store.wait()

    def z_take(index, value):
        near = (index + 1) // 2
        step = near + (1 - index % 2) * (NZ - 2 * near)
        z_copy(step).wait_recv()
        return value + zgot[step]

    final = lax.fori_loop(1, NZ, z_take, zsend[dx]) * (1.0 / (ORB * ATOMS * NZ * NY))
    sums_out[...] = final


def hand_over(filtered, sums, filt_out, corr_out, proj_out, held, held_sums, corr, proj, load_sem, store_sem):
    parts = [pl.ds(first, last - first) for first, last in ((0, 3), (3, 6), (6, 9), (9, ORB))]
    loads = [
        pltpu.make_async_copy(filtered.at[part], held.at[part], load_sem.at[index]) for index, part in enumerate(parts)
    ]
    stores = [
        pltpu.make_async_copy(held.at[part], filt_out.at[part], store_sem.at[index]) for index, part in enumerate(parts)
    ]
    load_sums = pltpu.make_async_copy(sums, held_sums, load_sem.at[4])
    load_sums.start()
    for load in loads:
        load.start()
    stores.append(pltpu.make_async_copy(corr, corr_out, store_sem.at[4]))
    stores.append(pltpu.make_async_copy(proj, proj_out, store_sem.at[5]))
    load_sums.wait()
    corr[...] = held_sums[:, 0:VEC]
    proj[...] = held_sums[:, VEC:]
    stores[4].start()
    stores[5].start()
    for load, store in zip(loads, stores):
        load.wait()
        store.start()
    for store in stores:
        store.wait()


def on_device(vectors, inner_pairs, inner_count, inner_blocks, cross_x_blocks, cross_y_blocks, spectrum_top, filter_cut):
    any_spec = pl.BlockSpec(memory_space=pl.ANY)
    hbm_spec = pl.BlockSpec(memory_space=pltpu.HBM)
    vmem_spec = pl.BlockSpec(memory_space=pltpu.VMEM)
    dma = pltpu.SemaphoreType.DMA
    block = jax.ShapeDtypeStruct((ORB, VEC, ATOMS), BF16)
    small = jax.ShapeDtypeStruct((8, VEC), F32)
    filtered, sums = pl.pallas_call(
        kernel,
        out_shape=(block, jax.ShapeDtypeStruct((8, ATOMS), F32)),
        in_specs=[hbm_spec] * 8,
        out_specs=(any_spec, vmem_spec),
        scratch_shapes=[
            pltpu.VMEM((5, ORB, VEC, ATOMS), BF16),
            pltpu.SMEM((1,), F32),
            pltpu.SMEM((1,), F32),
            pltpu.VMEM((SLOTS, ATOMS), jnp.int32),
            pltpu.VMEM((ATOMS,), jnp.int32),
            pltpu.VMEM((SLOTS, ORB, ORB, ATOMS), BF16),
            pltpu.VMEM((2, ORB, ORB, REACH, EDGE), BF16),
            pltpu.VMEM((ORB, ORB, 8, ATOMS), F32),
            pltpu.VMEM((8, ATOMS), jnp.int32),
            pltpu.VMEM((SLOTS, 8, ATOMS), F32),
            pltpu.VMEM((SLOTS, EDGE, ATOMS), F32),
            pltpu.VMEM((WIDE, WIDE), BF16),
            pltpu.VMEM((WIDE, WIDE), BF16),
            pltpu.VMEM((2, 2 * ATOMS, 2 * ATOMS), BF16),
            pltpu.VMEM((2, 2 * ATOMS, 2 * ATOMS), BF16),
            pltpu.VMEM((2, VEC, 2 * ATOMS), F32),
            pltpu.VMEM((2, VEC, 2 * ATOMS), BF16),
            pltpu.VMEM((2, VEC, 2 * ATOMS), BF16),
            pltpu.VMEM((4, 4, VEC, 2 * ATOMS), BF16),
            pltpu.VMEM((4, 4, VEC, 2 * ATOMS), BF16),
            pltpu.VMEM((ORB, VEC, ATOMS), F32),
            pltpu.VMEM((4, VEC, 2 * ATOMS), F32),
            pltpu.VMEM((4, VEC, 2 * ATOMS), F32),
            pltpu.VMEM((ORB, 4 * VEC, ATOMS), BF16),
            pltpu.VMEM((ORB, VEC, ATOMS), BF16),
            pltpu.VMEM((ORB, VEC, ATOMS), BF16),
            pltpu.VMEM((ORB, VEC, ATOMS), BF16),
            pltpu.VMEM((NY, 2, VEC, ATOMS), BF16),
            pltpu.VMEM((2 * NY, VEC, ATOMS), BF16),
            pltpu.VMEM((NZ, 8, ATOMS), F32),
            pltpu.VMEM((NZ, 8, ATOMS), F32),
            dma((8,)), dma(()), dma((2,)), dma((2,)), dma((4, 4)), dma((4, 4)), dma((10,)), dma((10,)),
            dma((2,)), dma((2,)), dma((2, 2 * NY)), dma((2, 2 * NY)), dma((NZ,)), dma((NZ,)),
        ],
        compiler_params=pltpu.CompilerParams(
            collective_id=0, has_side_effects=True, vmem_limit_bytes=VMEM_BYTES
        ),
        name="chebyshev",
    )(
        vectors, inner_pairs, inner_count, inner_blocks,
        cross_x_blocks.transpose(1, 2, 0, 3), cross_y_blocks.transpose(1, 2, 0, 3), spectrum_top, filter_cut,
    )
    filtered, correlation, projected = pl.pallas_call(
        hand_over,
        out_shape=(block, small, small),
        in_specs=[any_spec, any_spec],
        out_specs=(any_spec, any_spec, any_spec),
        scratch_shapes=[
            pltpu.VMEM((ORB, VEC, ATOMS), BF16), pltpu.VMEM((8, ATOMS), F32), pltpu.VMEM((8, VEC), F32),
            pltpu.VMEM((8, VEC), F32), dma((5,)), dma((6,)),
        ],
        compiler_params=pltpu.CompilerParams(vmem_limit_bytes=VMEM_BYTES),
        name="hand_over",
    )(filtered, sums)
    return filtered, correlation.T, projected.T


def solution(mesh):
    in_specs = (
        P(None, "band", ("dx", "dy")),
        P(None, ("dx", "dy")),
        P(("dx", "dy")),
        P(None, None, None, ("dx", "dy")),
        P(None, None, None, ("dx", "dy")),
        P(None, None, None, ("dx", "dy")),
        P(),
        P(),
    )
    out_specs = (P(None, "band", ("dx", "dy")), P("band", ("dx", "dy")), P("band", ("dx", "dy")))
    return jax.shard_map(on_device, mesh=mesh, in_specs=in_specs, out_specs=out_specs, check_vma=False)
```
